32 devices in a mesh: row: 4 (over z), col: 8 (over y, x, core).
Axes of the slice: x: 2, y: 2, z: 4, core: 2. Of those that a mesh axis runs over, the one named last changes fastest.
Arguments:
- query_vectors: bfloat16 [2048, 8, 128], P('col', 'row'), may hold values from -68 to 68
- key_vectors: bfloat16 [2048, 8, 128], P('col', 'row'), may hold values from -6 to 6
- value_vectors: bfloat16 [2048, 8, 128], P('col', 'row'), may hold values from -6 to 6
- gate_logits: bfloat16 [2048, 8, 128], P('col', 'row'), may hold values from -6 to 6
- cotangent: bfloat16 [2048, 8, 128], P('col', 'row'), may hold values from -6 to 6
- pair_bias: bfloat16 [16, 4, 128, 16, 128], P('col'), may hold values from -6 to 6
- block_table: int32 [16, 16], P('col'), may hold values from 0 to 15, as said below
- valid_counts: int32 [16], P('col'), may hold values from 1 to 16
Outputs:
- query_grad: bfloat16 [2048, 8, 128], P('col', 'row')
- key_grad: bfloat16 [2048, 8, 128], P('col', 'row')
- value_grad: bfloat16 [2048, 8, 128], P('col', 'row')
- gate_grad: bfloat16 [2048, 8, 128], P('col', 'row')
- bias_grad: bfloat16 [16, 4, 128, 16, 128], P('col', None, None, 'row')
The draws below stay inside these ranges and needn't reach their ends.
Inputs may be any that keep to these rules, and one draw needn't show every extreme that they name: `block_table`: each row holds 16 distinct block numbers; its first entry is the row's own block number.
All inputs are finite; a program needn't handle non-finite values.
Results may differ from the reference program's by a relative error of at most 0.03.
Values may be sent and summed in bfloat16 or wider, within the bound.
A program may use at most 128 MiB of HBM per device.

```python
import jax
import jax.numpy as jnp
from jax import lax

C = 128
H = 4
DH = 32
BS = 128
TAB = 16
I_DEV = 2
JB_DEV = 2
N = 2048
NB = 16
ROWS = 8
N_ROW = 4
N_COL = 8


def drawn_keys(key):
    base = jax.random.fold_in(key, 101)
    drawn = jnp.clip(jax.random.normal(base, (N, ROWS, C), jnp.float32), -6.0, 6.0)
    return drawn


def draw_key_vectors(key, part):
    drawn = drawn_keys(key)
    return drawn.astype(jnp.bfloat16)


def draw_query_vectors(key, part):
    noise_key = jax.random.fold_in(key, 103)
    result = jnp.clip(jax.random.normal(noise_key, (N, ROWS, C), jnp.float32), -6.0, 6.0)
    return result.astype(jnp.bfloat16)


def draw_block_table(key, part):
    row_keys = jax.random.split(jax.random.fold_in(key, 201), NB)
    shifts = jax.vmap(lambda single: jax.random.permutation(single, NB - 1))(row_keys)[:, :TAB - 1] + 1
    own = jnp.arange(NB, dtype=jnp.int32)[:, None]
    return jnp.concatenate([own, (own + shifts) % NB], axis=1).astype(jnp.int32)


def draw_valid_counts(key, part):
    counts = jax.random.randint(jax.random.fold_in(key, 301), (NB,), 1, TAB + 1)
    fullest = jax.random.randint(jax.random.fold_in(key, 302), (), 0, NB)
    shortest = (fullest + 1 + jax.random.randint(jax.random.fold_in(key, 303), (), 0, NB - 1)) % NB
    position = jnp.arange(NB)
    counts = jnp.where(position == fullest, TAB, counts)
    counts = jnp.where(position == shortest, 1, counts)
    return counts.astype(jnp.int32)


def level_of(key, shape, cuts, least, largest):
    def one(dim, blocks):
        heights = jax.random.uniform(jax.random.fold_in(jax.random.fold_in(key, 6), dim), (blocks,), jnp.float32, least / len(cuts), largest / len(cuts))
        return jnp.repeat(jnp.exp(heights), shape[dim] // blocks).reshape((-1,) + (1,) * (len(shape) - dim - 1))

    gain = one(*cuts[0])
    for cut in cuts[1:]:
        gain = gain * one(*cut)
    return gain


def centred(own_key, dims, spread, bound, pieces=(), held_as=jnp.bfloat16):
    values = jax.random.normal(own_key, dims, jnp.float32) * spread
    if len(pieces) > 0:
        values = level_of(own_key, dims, pieces, -0.22, 0.18) * values
    return jnp.clip(values, min=-bound, max=bound).astype(held_as)


def setup_inputs(seed: int = 0) -> dict:
    key_list = jax.random.split(jax.random.key(seed), 9)
    return {
        "query_vectors": draw_query_vectors(jax.random.fold_in(key_list[8], 71), 0),
        "key_vectors": draw_key_vectors(jax.random.fold_in(key_list[8], 71), 0),
        "value_vectors": centred(key_list[2], (N, ROWS, C), 1.0, 6.0, ((0, 8), (1, 4))),
        "gate_logits": centred(key_list[3], (N, ROWS, C), 1.5, 6.0, ((0, 8), (1, 4))),
        "cotangent": centred(key_list[4], (N, ROWS, C), 1.0, 6.0, ((0, 8), (1, 4))),
        "pair_bias": centred(key_list[5], (NB, H, BS, TAB, BS), 1.0, 6.0, ((0, 8),)),
        "block_table": draw_block_table(jax.random.fold_in(key_list[8], 71), 0),
        "valid_counts": draw_valid_counts(jax.random.fold_in(key_list[8], 71), 0),
    }


def block_terms(query_blk, gate_blk, upstream_blk, key_blk, value_blk, bias_blk, valid_count):
    row_count = query_blk.shape[1]
    extent = key_blk.shape[0]
    scale = DH ** -0.5
    query_four = query_blk.astype(jnp.float32).reshape(BS, row_count, H, DH)
    key_four = key_blk.astype(jnp.float32).reshape(extent, row_count, H, DH)
    value_four = value_blk.astype(jnp.float32).reshape(extent, row_count, H, DH)
    scores = jnp.einsum("qihd,kihd->ihqk", query_four, key_four) * scale
    scores = scores + bias_blk.astype(jnp.float32).reshape(H, BS, extent)[None]
    valid = (jnp.arange(extent) // BS) < valid_count
    scores = jnp.where(valid, scores, -jnp.inf)
    maxima = jnp.max(scores, axis=-1, keepdims=True)
    exponent = jnp.exp(scores - maxima)
    probability = exponent / jnp.sum(exponent, axis=-1, keepdims=True)
    weights = lax.optimization_barrier(probability.astype(jnp.bfloat16)).astype(jnp.float32)
    attended = jnp.einsum("ihqk,kihd->qihd", weights, value_four)
    opened = jax.nn.sigmoid(gate_blk.astype(jnp.float32)).reshape(BS, row_count, H, DH)
    upstream = upstream_blk.astype(jnp.float32).reshape(BS, row_count, H, DH)
    gate_grad = (upstream * attended * opened * (1.0 - opened)).reshape(BS, row_count, H * DH).astype(jnp.bfloat16)
    core_grad = lax.optimization_barrier((upstream * opened).astype(jnp.bfloat16)).astype(jnp.float32)
    offset = jnp.einsum("qihd,qihd->ihq", core_grad, attended)[..., None]
    weight_grad = jnp.einsum("qihd,kihd->ihqk", core_grad, value_four)
    score_grad = probability * (weight_grad - offset)
    score_half = lax.optimization_barrier(score_grad.astype(jnp.bfloat16)).astype(jnp.float32)
    query_grad = (jnp.einsum("ihqk,kihd->qihd", score_half, key_four) * scale).reshape(BS, row_count, H * DH).astype(jnp.bfloat16)
    key_term = jnp.einsum("ihqk,qihd->kihd", score_half, query_four) * scale
    value_term = jnp.einsum("ihqk,qihd->kihd", weights, core_grad)
    return query_grad, gate_grad, key_term.reshape(extent, row_count, H * DH), value_term.reshape(extent, row_count, H * DH), score_grad


def reference(query_vectors, key_vectors, value_vectors, gate_logits, cotangent, pair_bias, block_table, valid_counts):
    row_count = query_vectors.shape[1]
    key_blocks = key_vectors.reshape(NB, BS, row_count, C)
    value_blocks = value_vectors.reshape(NB, BS, row_count, C)

    def group_step(carry, group):
        key_total, value_total = carry
        key_acc = jnp.zeros((NB, BS, row_count, C), jnp.float32)
        value_acc = jnp.zeros((NB, BS, row_count, C), jnp.float32)
        query_parts = []
        gate_parts = []
        bias_parts = []
        for local in range(JB_DEV):
            block = (group * JB_DEV + local).astype(jnp.int32)
            start = (block * BS).astype(jnp.int32)
            query_blk = lax.dynamic_slice_in_dim(query_vectors, start, BS, 0)
            gate_blk = lax.dynamic_slice_in_dim(gate_logits, start, BS, 0)
            upstream_blk = lax.dynamic_slice_in_dim(cotangent, start, BS, 0)
            block_ids = lax.dynamic_index_in_dim(block_table, block, 0, keepdims=False).astype(jnp.int32)
            valid_count = lax.dynamic_index_in_dim(valid_counts, block, 0, keepdims=False)
            bias_blk = lax.dynamic_index_in_dim(pair_bias, block, 0, keepdims=False)
            key_blk = jnp.take(key_blocks, block_ids, axis=0).reshape(TAB * BS, row_count, C)
            value_blk = jnp.take(value_blocks, block_ids, axis=0).reshape(TAB * BS, row_count, C)
            query_grad, gate_grad, key_term, value_term, score_grad = block_terms(query_blk, gate_blk, upstream_blk, key_blk, value_blk, bias_blk, valid_count)
            key_acc = key_acc.at[block_ids].add(key_term.reshape(TAB, BS, row_count, C))
            value_acc = value_acc.at[block_ids].add(value_term.reshape(TAB, BS, row_count, C))
            row_partial = score_grad.reshape(N_ROW, I_DEV, H, BS, TAB * BS).sum(axis=1)
            row_partial = lax.optimization_barrier(row_partial.astype(jnp.bfloat16)).astype(jnp.float32)
            bias_parts.append(row_partial.sum(axis=0).reshape(H, BS, TAB, BS).astype(jnp.bfloat16))
            query_parts.append(query_grad)
            gate_parts.append(gate_grad)
        key_total = key_total + lax.optimization_barrier(key_acc.astype(jnp.bfloat16)).astype(jnp.float32)
        value_total = value_total + lax.optimization_barrier(value_acc.astype(jnp.bfloat16)).astype(jnp.float32)
        outputs = (jnp.concatenate(query_parts, 0), jnp.concatenate(gate_parts, 0), jnp.stack(bias_parts, 0))
        return (key_total, value_total), outputs

    initial = (jnp.zeros((NB, BS, row_count, C), jnp.float32), jnp.zeros((NB, BS, row_count, C), jnp.float32))
    groups = jnp.arange(N_COL, dtype=jnp.int32)
    totals, stacked = lax.scan(group_step, initial, groups)
    key_grad = totals[0].reshape(N, row_count, C).astype(jnp.bfloat16)
    value_grad = totals[1].reshape(N, row_count, C).astype(jnp.bfloat16)
    query_grad = stacked[0].reshape(N, row_count, C)
    gate_grad = stacked[1].reshape(N, row_count, C)
    bias_grad = stacked[2].reshape(NB, H, BS, TAB, BS)
    return query_grad, key_grad, value_grad, gate_grad, bias_grad
```

```python
import functools

import jax
import jax.numpy as jnp
from jax import lax
from jax.experimental import pallas as pl
from jax.experimental.pallas import tpu as pltpu
from jax.sharding import PartitionSpec as P

H = 4
DH = 32
BS = 128
TAB = 16
PAIRS = TAB // 2
C = H * DH
HQ = H * BS
SCALE = DH ** (-0.5)
LOG2E = 1.4426950408889634
F32 = jnp.float32
BF16 = jnp.bfloat16
NT = (((1,), (1,)), ((), ()))
NN = (((1,), (0,)), ((), ()))


def dot(a, b, dims=NN):
    return lax.dot_general(a, b, dims, preferred_element_type=F32)


def attention_kernel(rows, last, *refs):
    (tab_k, tab_v, count, q_ref, g_ref, c_ref, k_ref, v_ref, b_ref), refs = refs[:9], refs[9:]
    if last:
        (dk_in, dv_in), refs = refs[:2], refs[2:]
    (dq_ref, gg_ref, bg_ref, dk_out, dv_out), refs = refs[:5], refs[5:]
    s_ref, e_ref, qm, cm, qt, ct, mx, att, off, dqa = refs[:10]
    if last:
        dk_ref, dv_ref = refs[10:]
        dk_ref[...] = dk_in[...]
        dv_ref[...] = dv_in[...]
    else:
        dk_ref, dv_ref = dk_out, dv_out
        dk_ref[...] = jnp.zeros_like(dk_ref)
        dv_ref[...] = jnp.zeros_like(dv_ref)
    valid = count[0]
    pairs = (valid + 1) // 2
    lane_head = lax.broadcasted_iota(jnp.int32, (BS, C), 1) // DH

    def per_head(x):
        return jnp.concatenate([jnp.where(lane_head == h, x, 0.0) for h in range(H)], 0)

    def merge_heads(x):
        total = jnp.zeros((BS, C), F32)
        for h in range(H):
            total = jnp.where(lane_head == h, x[h * BS : (h + 1) * BS], total)
        return total

    def store_transposed(dst, i, x):
        for hp in range(2):
            turned = jnp.transpose(x[hp * 256 : (hp + 1) * 256])
            dst[i, hp] = turned[hp * 64 : (hp + 1) * 64].astype(BF16)

    def two(ref, tab, p, i):
        lanes = slice(i * C, (i + 1) * C)
        return jnp.concatenate([ref[tab[2 * p], :, lanes], ref[tab[2 * p + 1], :, lanes]], 0)

    def wide(x):
        return jnp.concatenate([x, x], 1)

    for i in range(rows):
        q_heads = per_head(q_ref[:, i * C : (i + 1) * C].astype(F32))
        qm[i] = q_heads.astype(BF16)
        store_transposed(qt, i, q_heads)
        mx[i] = jnp.full((HQ, 128), -jnp.inf, F32)
        att[i] = jnp.zeros((HQ, 256), F32)
        dqa[i] = jnp.zeros((HQ, C), F32)

    @pl.loop(0, pairs)
    def _(p):
        lane_slot = lax.broadcasted_iota(jnp.int32, (1, 2 * BS), 1) // BS
        shut = jnp.where(2 * p + lane_slot < valid, 0.0, -jnp.inf)
        bias = b_ref[p].astype(F32) * LOG2E + shut
        for i in range(rows):
            raw = dot(qm[i], two(k_ref, tab_k, p, i), NT)
            s = raw * (SCALE * LOG2E) + bias
            s_ref[p, i] = s
            mx[i] = jnp.maximum(mx[i], jnp.maximum(s[:, :BS], s[:, BS:]))

    for i in range(rows):
        mx[i] = jnp.broadcast_to(jnp.max(mx[i], axis=1, keepdims=True), (HQ, 128))

    @pl.loop(0, pairs)
    def _(p):
        for i in range(rows):
            e = jnp.exp2(s_ref[p, i] - wide(mx[i])).astype(BF16)
            e_ref[p, i] = e
            values = jnp.concatenate([two(v_ref, tab_v, p, i), jnp.ones((2 * BS, C), BF16)], 1)
            att[i] += dot(e, values)

    for i in range(rows):
        lanes = slice(i * C, (i + 1) * C)
        inverse = 1.0 / att[i, :, C:]
        attended = att[i, :, :C] * inverse
        opened = jax.nn.sigmoid(g_ref[:, lanes].astype(F32))
        upstream = c_ref[:, lanes].astype(F32)
        gg_ref[:, lanes] = (upstream * merge_heads(attended) * opened * (1.0 - opened)).astype(BF16)
        core = (upstream * opened).astype(BF16).astype(F32)
        core_scaled = (per_head(core) * inverse).astype(BF16)
        cm[i] = core_scaled
        scaled = core_scaled.astype(F32)
        store_transposed(ct, i, scaled)
        off[i] = jnp.broadcast_to(jnp.sum(scaled * attended, axis=1, keepdims=True), (HQ, 128))

    @pl.loop(0, pairs)
    def _(p):
        total = None
        for i in range(rows):
            keys = two(k_ref, tab_k, p, i)
            dw = dot(cm[i], two(v_ref, tab_v, p, i), NT)
            e = e_ref[p, i]
            ds = e.astype(F32) * (dw - wide(off[i]))
            total = ds if total is None else total + ds
            half = ds.astype(BF16)
            dqa[i] += dot(half, keys)
            for hp in range(2):
                span = slice(hp * 256, (hp + 1) * 256)
                dst = slice(i * C + hp * 64, i * C + (hp + 1) * 64)
                key_term = dot(qt[i, hp], half[span])
                value_term = dot(ct[i, hp], e[span])
                for slot in range(2):
                    part = slice(slot * BS, (slot + 1) * BS)
                    dk_ref[tab_k[2 * p + slot], dst, :] += key_term[:, part]
                    dv_ref[tab_v[2 * p + slot], dst, :] += value_term[:, part]
        bg_ref[p] = total.astype(BF16)

    @pl.loop(pairs, PAIRS)
    def _(p):
        bg_ref[p] = jnp.zeros((HQ, 2 * BS), BF16)

    for i in range(rows):
        dq_ref[:, i * C : (i + 1) * C] = (merge_heads(dqa[i]) * SCALE).astype(BF16)
    if last:

        @pl.loop(0, dk_ref.shape[0])
        def _(b):
            dk_out[b] = (dk_ref[b] * SCALE).astype(BF16)
            dv_out[b] = dv_ref[b].astype(BF16)


def attention(rows, last, tab_k, tab_v, count, q, g, c, k, v, b, sums):
    blocks = k.shape[0]
    width = rows * C
    smem = pl.BlockSpec(memory_space=pltpu.SMEM)
    vmem = pl.BlockSpec(memory_space=pltpu.VMEM)
    acc = pltpu.VMEM((blocks, width, BS), F32)
    scratch = [
        pltpu.VMEM((PAIRS, rows, HQ, 2 * BS), F32),
        pltpu.VMEM((PAIRS, rows, HQ, 2 * BS), BF16),
        pltpu.VMEM((rows, HQ, C), BF16),
        pltpu.VMEM((rows, HQ, C), BF16),
        pltpu.VMEM((rows, 2, 64, 256), BF16),
        pltpu.VMEM((rows, 2, 64, 256), BF16),
        pltpu.VMEM((rows, HQ, 128), F32),
        pltpu.VMEM((rows, HQ, 256), F32),
        pltpu.VMEM((rows, HQ, 128), F32),
        pltpu.VMEM((rows, HQ, C), F32),
    ]
    sum_type = BF16 if last else F32
    return pl.pallas_call(
        functools.partial(attention_kernel, rows, last),
        out_shape=(
            jax.ShapeDtypeStruct((BS, width), BF16),
            jax.ShapeDtypeStruct((BS, width), BF16),
            jax.ShapeDtypeStruct((PAIRS, HQ, 2 * BS), BF16),
            jax.ShapeDtypeStruct((blocks, width, BS), sum_type),
            jax.ShapeDtypeStruct((blocks, width, BS), sum_type),
        ),
        in_specs=[smem] * 3 + [vmem] * (6 + len(sums)),
        out_specs=[vmem] * 5,
        scratch_shapes=scratch + ([acc, acc] if last else []),
        compiler_params=pltpu.CompilerParams(vmem_limit_bytes=56 * 1024 * 1024),
        cost_estimate=pl.CostEstimate(
            flops=6 * 2 * rows * HQ * TAB * BS * 256,
            bytes_accessed=12 * 1024 * 1024,
            transcendentals=rows * HQ * TAB * BS,
        ),
    )(tab_k, tab_v, count, q, g, c, k, v, b, *sums)


def exchange(x, bit, size):
    return lax.ppermute(x, "col", [(d, d ^ bit) for d in range(size)])


def gather(x, order, size):
    for bit in order:
        x = jnp.concatenate([x, exchange(x, bit, size)], 0)
    return x


def scatter_sum(x, order, size):
    for bit in reversed(order):
        half = x.shape[0] // 2
        got = exchange(x[half:], bit, size)
        x = (x[:half].astype(F32) + got.astype(F32)).astype(BF16)
    return x


def positions(blocks, order, me, per_device):
    apart = (blocks // per_device) ^ me
    place = jnp.zeros_like(apart)
    for rank, bit in enumerate(order):
        place = place + jnp.where((apart & bit) != 0, 1 << rank, 0)
    return place * per_device + blocks % per_device


def body(q, k, v, g, c, pair_bias, block_table, valid_counts):
    length, rows, channels = q.shape
    local = length // BS
    width = rows * channels
    size = lax.axis_size("col")
    me = lax.axis_index("col")
    bits = [1 << n for n in range(size.bit_length() - 1)]
    order_k = bits[1:] + bits[:1]
    order_v = bits[1:][::-1] + bits[:1]
    k_all = gather(k.reshape(local, BS, width), order_k, size)
    v_all = gather(v.reshape(local, BS, width), order_v, size)
    tab_k = positions(block_table, order_k, me, local)
    tab_v = positions(block_table, order_v, me, local)
    q, g, c = (x.reshape(local, BS, width) for x in (q, g, c))
    bias = pair_bias.reshape(local, HQ, PAIRS, 2 * BS).transpose(0, 2, 1, 3)
    sums = ()
    dqs, ggs, biases = [], [], []
    for j in range(local):
        dq, gg, bg, *sums = attention(
            rows, j == local - 1, tab_k[j], tab_v[j], valid_counts[j : j + 1],
            q[j], g[j], c[j], k_all, v_all, bias[j], sums,
        )
        dqs.append(dq)
        ggs.append(gg)
        biases.append(lax.psum_scatter(bg, "row", scatter_dimension=0, tiled=True))
    dk = scatter_sum(sums[0], order_k, size)
    dv = scatter_sum(sums[1], order_v, size)

    def leave(x):
        return x.transpose(0, 2, 1).reshape(length, rows, channels)

    own = biases[0].shape[0]
    bias_grad = jnp.stack(biases, 0).reshape(local, own, H, BS, 2, BS)
    bias_grad = bias_grad.transpose(0, 2, 3, 1, 4, 5).reshape(local, H, BS, own * 2, BS)
    return (
        jnp.concatenate(dqs, 0).reshape(length, rows, channels),
        leave(dk),
        leave(dv),
        jnp.concatenate(ggs, 0).reshape(length, rows, channels),
        bias_grad,
    )


def solution(mesh):
    split = P("col", "row", None)
    bias = P("col", None, None, None, None)
    return jax.shard_map(
        body,
        mesh=mesh,
        in_specs=(split,) * 5 + (bias, P("col", None), P("col")),
        out_specs=(split,) * 4 + (P("col", None, None, "row", None),),
        check_vma=False,
    )
```

```python
import functools

import jax
import jax.numpy as jnp
from jax import lax
from jax.experimental import pallas as pl
from jax.experimental.pallas import tpu as pltpu
from jax.sharding import PartitionSpec as P

H = 4
DH = 32
BS = 128
TAB = 16
PAIRS = TAB // 2
C = H * DH
HQ = H * BS
SCALE = DH ** (-0.5)
LOG2E = 1.4426950408889634
F32 = jnp.float32
BF16 = jnp.bfloat16
NT = (((1,), (1,)), ((), ()))
NN = (((1,), (0,)), ((), ()))


def dot(a, b, dims=NN):
    return lax.dot_general(a, b, dims, preferred_element_type=F32)


def attention_kernel(rows, last, *refs):
    (tab_k, tab_v, count, q_ref, g_ref, c_ref, k_ref, v_ref, b_ref), refs = refs[:9], refs[9:]
    if last:
        (dk_in, dv_in), refs = refs[:2], refs[2:]
    (dq_ref, gg_ref, bg_ref, dk_out, dv_out), refs = refs[:5], refs[5:]
    s_ref, e_ref, qm, cm, qt, ct, mx, att, off, dqa, bias_ref = refs[:11]
    if last:
        dk_ref, dv_ref = refs[11:]
        dk_ref[...] = dk_in[...]
        dv_ref[...] = dv_in[...]
    else:
        dk_ref, dv_ref = dk_out, dv_out
        dk_ref[...] = jnp.zeros_like(dk_ref)
        dv_ref[...] = jnp.zeros_like(dv_ref)
    valid = count[0]
    pairs = (valid + 1) // 2
    lane_head = lax.broadcasted_iota(jnp.int32, (BS, C), 1) // DH

    def per_head(x):
        return jnp.concatenate([jnp.where(lane_head == h, x, 0.0) for h in range(H)], 0)

    def merge_heads(x):
        total = jnp.zeros((BS, C), F32)
        for h in range(H):
            total = jnp.where(lane_head == h, x[h * BS : (h + 1) * BS], total)
        return total

    def store_transposed(dst, i, x):
        for hp in range(2):
            turned = jnp.transpose(x[hp * 256 : (hp + 1) * 256])
            dst[i, hp] = turned[hp * 64 : (hp + 1) * 64].astype(BF16)

    def two(ref, tab, p, i):
        lanes = slice(i * C, (i + 1) * C)
        return jnp.concatenate([ref[tab[2 * p], :, lanes], ref[tab[2 * p + 1], :, lanes]], 0)

    def wide(x):
        return jnp.concatenate([x, x], 1)

    for h in range(H):
        span = slice(h * BS * TAB, (h + 1) * BS * TAB)
        bias_ref[span] = b_ref[h].reshape(BS * TAB, BS).astype(F32) * LOG2E

    for i in range(rows):
        q_heads = per_head(q_ref[:, i * C : (i + 1) * C].astype(F32))
        qm[i] = q_heads.astype(BF16)
        store_transposed(qt, i, q_heads)
        mx[i] = jnp.full((HQ, 128), -jnp.inf, F32)
        att[i] = jnp.zeros((HQ, 256), F32)
        dqa[i] = jnp.zeros((HQ, C), F32)

    @pl.loop(0, pairs)
    def _(p):
        lane_slot = lax.broadcasted_iota(jnp.int32, (1, 2 * BS), 1) // BS
        shut = jnp.where(2 * p + lane_slot < valid, 0.0, -jnp.inf)
        first = bias_ref[pl.ds(2 * p, HQ, stride=TAB), :]
        second = bias_ref[pl.ds(2 * p + 1, HQ, stride=TAB), :]
        bias = jnp.concatenate([first, second], 1) + shut
        for i in range(rows):
            raw = dot(qm[i], two(k_ref, tab_k, p, i), NT)
            s = raw * (SCALE * LOG2E) + bias
            s_ref[p, i] = s
            mx[i] = jnp.maximum(mx[i], jnp.maximum(s[:, :BS], s[:, BS:]))

    for i in range(rows):
        mx[i] = jnp.broadcast_to(jnp.max(mx[i], axis=1, keepdims=True), (HQ, 128))

    @pl.loop(0, pairs)
    def _(p):
        for i in range(rows):
            e = jnp.exp2(s_ref[p, i] - wide(mx[i])).astype(BF16)
            e_ref[p, i] = e
            values = jnp.concatenate([two(v_ref, tab_v, p, i), jnp.ones((2 * BS, C), BF16)], 1)
            att[i] += dot(e, values)

    for i in range(rows):
        lanes = slice(i * C, (i + 1) * C)
        inverse = 1.0 / att[i, :, C:]
        attended = att[i, :, :C] * inverse
        opened = jax.nn.sigmoid(g_ref[:, lanes].astype(F32))
        upstream = c_ref[:, lanes].astype(F32)
        gg_ref[:, lanes] = (upstream * merge_heads(attended) * opened * (1.0 - opened)).astype(BF16)
        core = (upstream * opened).astype(BF16).astype(F32)
        core_scaled = (per_head(core) * inverse).astype(BF16)
        cm[i] = core_scaled
        scaled = core_scaled.astype(F32)
        store_transposed(ct, i, scaled)
        off[i] = jnp.broadcast_to(jnp.sum(scaled * attended, axis=1, keepdims=True), (HQ, 128))

    @pl.loop(0, pairs)
    def _(p):
        total = None
        for i in range(rows):
            keys = two(k_ref, tab_k, p, i)
            dw = dot(cm[i], two(v_ref, tab_v, p, i), NT)
            e = e_ref[p, i]
            ds = e.astype(F32) * (dw - wide(off[i]))
            total = ds if total is None else total + ds
            half = ds.astype(BF16)
            dqa[i] += dot(half, keys)
            for hp in range(2):
                span = slice(hp * 256, (hp + 1) * 256)
                dst = slice(i * C + hp * 64, i * C + (hp + 1) * 64)
                key_term = dot(qt[i, hp], half[span])
                value_term = dot(ct[i, hp], e[span])
                for slot in range(2):
                    part = slice(slot * BS, (slot + 1) * BS)
                    dk_ref[tab_k[2 * p + slot], dst, :] += key_term[:, part]
                    dv_ref[tab_v[2 * p + slot], dst, :] += value_term[:, part]
        bg_ref[p] = total.astype(BF16)

    @pl.loop(pairs, PAIRS)
    def _(p):
        bg_ref[p] = jnp.zeros((HQ, 2 * BS), BF16)

    for i in range(rows):
        dq_ref[:, i * C : (i + 1) * C] = (merge_heads(dqa[i]) * SCALE).astype(BF16)
    if last:

        @pl.loop(0, dk_ref.shape[0])
        def _(b):
            dk_out[b] = (dk_ref[b] * SCALE).astype(BF16)
            dv_out[b] = dv_ref[b].astype(BF16)


def attention(rows, j, last, tab_k, tab_v, count, q, g, c, k, v, b, sums):
    blocks = k.shape[0]
    width = rows * C
    smem = pl.BlockSpec(memory_space=pltpu.SMEM)
    vmem = pl.BlockSpec(memory_space=pltpu.VMEM)
    block = pl.BlockSpec((None, BS, width), lambda n: (j, 0, 0))
    bias_block = pl.BlockSpec((None, H, BS, TAB, BS), lambda n: (j, 0, 0, 0, 0))
    acc = pltpu.VMEM((blocks, width, BS), F32)
    scratch = [
        pltpu.VMEM((PAIRS, rows, HQ, 2 * BS), F32),
        pltpu.VMEM((PAIRS, rows, HQ, 2 * BS), BF16),
        pltpu.VMEM((rows, HQ, C), BF16),
        pltpu.VMEM((rows, HQ, C), BF16),
        pltpu.VMEM((rows, 2, 64, 256), BF16),
        pltpu.VMEM((rows, 2, 64, 256), BF16),
        pltpu.VMEM((rows, HQ, 128), F32),
        pltpu.VMEM((rows, HQ, 256), F32),
        pltpu.VMEM((rows, HQ, 128), F32),
        pltpu.VMEM((rows, HQ, C), F32),
        pltpu.VMEM((HQ * TAB, BS), F32),
    ]
    sum_type = BF16 if last else F32
    return pl.pallas_call(
        functools.partial(attention_kernel, rows, last),
        out_shape=(
            jax.ShapeDtypeStruct((BS, width), BF16),
            jax.ShapeDtypeStruct((BS, width), BF16),
            jax.ShapeDtypeStruct((PAIRS, HQ, 2 * BS), BF16),
            jax.ShapeDtypeStruct((blocks, width, BS), sum_type),
            jax.ShapeDtypeStruct((blocks, width, BS), sum_type),
        ),
        grid=(1,),
        in_specs=[smem] * 3 + [block] * 3 + [vmem] * 2 + [bias_block] + [vmem] * len(sums),
        out_specs=[vmem] * 5,
        scratch_shapes=scratch + ([acc, acc] if last else []),
        compiler_params=pltpu.CompilerParams(vmem_limit_bytes=56 * 1024 * 1024),
        cost_estimate=pl.CostEstimate(
            flops=6 * 2 * rows * HQ * TAB * BS * 256,
            bytes_accessed=12 * 1024 * 1024,
            transcendentals=rows * HQ * TAB * BS,
        ),
    )(tab_k, tab_v, count, q, g, c, k, v, b, *sums)


def exchange(x, bit, size):
    return lax.ppermute(x, "col", [(d, d ^ bit) for d in range(size)])


def gather(x, order, size):
    for bit in order:
        x = jnp.concatenate([x, exchange(x, bit, size)], 0)
    return x


def scatter_sum(x, order, size):
    for bit in reversed(order):
        half = x.shape[0] // 2
        got = exchange(x[half:], bit, size)
        x = (x[:half].astype(F32) + got.astype(F32)).astype(BF16)
    return x


def line_sum(x):
    size = lax.axis_size("row")
    me = lax.axis_index("row")
    share = x.shape[0] // size

    def own(owner):
        start = jnp.clip(owner, 0, size - 1) * share
        return lax.dynamic_slice_in_dim(x, start, share, 0).astype(F32)

    down = up = None
    for step in range(size - 1):
        down_term = own(me + step - (size - 1))
        up_term = own(me + (size - 1) - step)
        if step > 0:
            down_term = down_term + down.astype(F32)
            up_term = up_term + up.astype(F32)
        down_pairs = [(r, r - 1) for r in range(max(1, size - 1 - step), size)]
        up_pairs = [(r, r + 1) for r in range(min(size - 1, step + 1))]
        down = lax.ppermute(down_term.astype(BF16), "row", down_pairs)
        up = lax.ppermute(up_term.astype(BF16), "row", up_pairs)
    return (own(me) + down.astype(F32) + up.astype(F32)).astype(BF16)


def positions(blocks, order, me, per_device):
    apart = (blocks // per_device) ^ me
    place = jnp.zeros_like(apart)
    for rank, bit in enumerate(order):
        place = place + jnp.where((apart & bit) != 0, 1 << rank, 0)
    return place * per_device + blocks % per_device


def body(q, k, v, g, c, pair_bias, block_table, valid_counts):
    length, rows, channels = q.shape
    local = length // BS
    width = rows * channels
    size = lax.axis_size("col")
    me = lax.axis_index("col")
    bits = [1 << n for n in range(size.bit_length() - 1)]
    order_k = bits[1:] + bits[:1]
    order_v = bits[1:][::-1] + bits[:1]
    k_all = gather(k.reshape(local, BS, width), order_k, size)
    v_all = gather(v.reshape(local, BS, width), order_v, size)
    tab_k = positions(block_table, order_k, me, local)
    tab_v = positions(block_table, order_v, me, local)
    q, g, c = (x.reshape(local, BS, width) for x in (q, g, c))
    sums = ()
    dqs, ggs, terms = [], [], []
    for j in range(local):
        dq, gg, bg, *sums = attention(
            rows, j, j == local - 1, tab_k[j], tab_v[j], valid_counts[j : j + 1],
            q, g, c, k_all, v_all, pair_bias, sums,
        )
        dqs.append(dq)
        ggs.append(gg)
        terms.append(bg)
    biases = [line_sum(bg) for bg in terms]
    dk = scatter_sum(sums[0], order_k, size)
    dv = scatter_sum(sums[1], order_v, size)

    def leave(x):
        return x.transpose(0, 2, 1).reshape(length, rows, channels)

    own = biases[0].shape[0]
    bias_grad = jnp.stack(biases, 0).reshape(local, own, H, BS, 2, BS)
    bias_grad = bias_grad.transpose(0, 2, 3, 1, 4, 5).reshape(local, H, BS, own * 2, BS)
    return (
        jnp.concatenate(dqs, 0).reshape(length, rows, channels),
        leave(dk),
        leave(dv),
        jnp.concatenate(ggs, 0).reshape(length, rows, channels),
        bias_grad,
    )


def solution(mesh):
    split = P("col", "row", None)
    bias = P("col", None, None, None, None)
    return jax.shard_map(
        body,
        mesh=mesh,
        in_specs=(split,) * 5 + (bias, P("col", None), P("col")),
        out_specs=(split,) * 4 + (P("col", None, None, "row", None),),
        check_vma=False,
    )
```

```python
import functools

import jax
import jax.numpy as jnp
from jax import lax
from jax.experimental import pallas as pl
from jax.experimental.pallas import tpu as pltpu
from jax.sharding import PartitionSpec as P

H = 4
DH = 32
BS = 128
TAB = 16
PAIRS = TAB // 2
C = H * DH
HQ = H * BS
SCALE = DH ** (-0.5)
LOG2E = 1.4426950408889634
F32 = jnp.float32
BF16 = jnp.bfloat16
MESH = pl.DeviceIdType.MESH
NT = (((1,), (1,)), ((), ()))
NN = (((1,), (0,)), ((), ()))


def dot(a, b, dims=NN):
    return lax.dot_general(a, b, dims, preferred_element_type=F32)


def attention_kernel(rows, last, *refs):
    (tab_k, tab_v, count, q_ref, g_ref, c_ref, k_ref, v_ref, b_ref), refs = refs[:9], refs[9:]
    if last:
        (dk_in, dv_in), refs = refs[:2], refs[2:]
    (dq_ref, gg_ref, bg_ref, dk_out, dv_out), refs = refs[:5], refs[5:]
    s_ref, e_ref, qm, cm, qt, ct, mx, att, off, dqa, bias_ref = refs[:11]
    if last:
        dk_ref, dv_ref = refs[11:]
        dk_ref[...] = dk_in[...]
        dv_ref[...] = dv_in[...]
    else:
        dk_ref, dv_ref = dk_out, dv_out
        dk_ref[...] = jnp.zeros_like(dk_ref)
        dv_ref[...] = jnp.zeros_like(dv_ref)
    valid = count[0]
    pairs = (valid + 1) // 2
    lane_head = lax.broadcasted_iota(jnp.int32, (BS, C), 1) // DH

    def per_head(x):
        return jnp.concatenate([jnp.where(lane_head == h, x, 0.0) for h in range(H)], 0)

    def merge_heads(x):
        total = jnp.zeros((BS, C), F32)
        for h in range(H):
            total = jnp.where(lane_head == h, x[h * BS : (h + 1) * BS], total)
        return total

    def store_transposed(dst, i, x):
        for hp in range(2):
            turned = jnp.transpose(x[hp * 256 : (hp + 1) * 256])
            dst[i, hp] = turned[hp * 64 : (hp + 1) * 64].astype(BF16)

    def two(ref, tab, p, i):
        lanes = slice(i * C, (i + 1) * C)
        return jnp.concatenate([ref[tab[2 * p], :, lanes], ref[tab[2 * p + 1], :, lanes]], 0)

    def wide(x):
        return jnp.concatenate([x, x], 1)

    for h in range(H):
        span = slice(h * BS * TAB, (h + 1) * BS * TAB)
        bias_ref[span] = b_ref[h].reshape(BS * TAB, BS).astype(F32) * LOG2E

    for i in range(rows):
        q_heads = per_head(q_ref[:, i * C : (i + 1) * C].astype(F32))
        qm[i] = q_heads.astype(BF16)
        store_transposed(qt, i, q_heads)
        mx[i] = jnp.full((HQ, 128), -jnp.inf, F32)
        att[i] = jnp.zeros((HQ, 256), F32)
        dqa[i] = jnp.zeros((HQ, C), F32)

    @pl.loop(0, pairs)
    def _(p):
        lane_slot = lax.broadcasted_iota(jnp.int32, (1, 2 * BS), 1) // BS
        shut = jnp.where(2 * p + lane_slot < valid, 0.0, -jnp.inf)
        first = bias_ref[pl.ds(2 * p, HQ, stride=TAB), :]
        second = bias_ref[pl.ds(2 * p + 1, HQ, stride=TAB), :]
        bias = jnp.concatenate([first, second], 1) + shut
        for i in range(rows):
            raw = dot(qm[i], two(k_ref, tab_k, p, i), NT)
            s = raw * (SCALE * LOG2E) + bias
            s_ref[p, i] = s
            mx[i] = jnp.maximum(mx[i], jnp.maximum(s[:, :BS], s[:, BS:]))

    for i in range(rows):
        mx[i] = jnp.broadcast_to(jnp.max(mx[i], axis=1, keepdims=True), (HQ, 128))

    @pl.loop(0, pairs)
    def _(p):
        for i in range(rows):
            e = jnp.exp2(s_ref[p, i] - wide(mx[i])).astype(BF16)
            e_ref[p, i] = e
            values = jnp.concatenate([two(v_ref, tab_v, p, i), jnp.ones((2 * BS, C), BF16)], 1)
            att[i] += dot(e, values)

    for i in range(rows):
        lanes = slice(i * C, (i + 1) * C)
        inverse = 1.0 / att[i, :, C:]
        attended = att[i, :, :C] * inverse
        opened = jax.nn.sigmoid(g_ref[:, lanes].astype(F32))
        upstream = c_ref[:, lanes].astype(F32)
        gg_ref[:, lanes] = (upstream * merge_heads(attended) * opened * (1.0 - opened)).astype(BF16)
        core = (upstream * opened).astype(BF16).astype(F32)
        core_scaled = (per_head(core) * inverse).astype(BF16)
        cm[i] = core_scaled
        scaled = core_scaled.astype(F32)
        store_transposed(ct, i, scaled)
        off[i] = jnp.broadcast_to(jnp.sum(scaled * attended, axis=1, keepdims=True), (HQ, 128))

    @pl.loop(0, pairs)
    def _(p):
        total = None
        for i in range(rows):
            keys = two(k_ref, tab_k, p, i)
            dw = dot(cm[i], two(v_ref, tab_v, p, i), NT)
            e = e_ref[p, i]
            ds = e.astype(F32) * (dw - wide(off[i]))
            total = ds if total is None else total + ds
            half = ds.astype(BF16)
            dqa[i] += dot(half, keys)
            for hp in range(2):
                span = slice(hp * 256, (hp + 1) * 256)
                dst = slice(i * C + hp * 64, i * C + (hp + 1) * 64)
                key_term = dot(qt[i, hp], half[span])
                value_term = dot(ct[i, hp], e[span])
                for slot in range(2):
                    part = slice(slot * BS, (slot + 1) * BS)
                    dk_ref[tab_k[2 * p + slot], dst, :] += key_term[:, part]
                    dv_ref[tab_v[2 * p + slot], dst, :] += value_term[:, part]
        bg_ref[p] = total.astype(BF16)

    @pl.loop(pairs, PAIRS)
    def _(p):
        bg_ref[p] = jnp.zeros((HQ, 2 * BS), BF16)

    for i in range(rows):
        dq_ref[:, i * C : (i + 1) * C] = (merge_heads(dqa[i]) * SCALE).astype(BF16)
    if last:

        @pl.loop(0, dk_ref.shape[0])
        def _(b):
            dk_out[b] = (dk_ref[b] * SCALE).astype(BF16)
            dv_out[b] = dv_ref[b].astype(BF16)


def attention(rows, j, last, tab_k, tab_v, count, q, g, c, k, v, b, sums):
    blocks = k.shape[0]
    width = rows * C
    smem = pl.BlockSpec(memory_space=pltpu.SMEM)
    vmem = pl.BlockSpec(memory_space=pltpu.VMEM)
    block = pl.BlockSpec((None, BS, width), lambda n: (j, 0, 0))
    bias_block = pl.BlockSpec((None, H, BS, TAB, BS), lambda n: (j, 0, 0, 0, 0))
    acc = pltpu.VMEM((blocks, width, BS), F32)
    scratch = [
        pltpu.VMEM((PAIRS, rows, HQ, 2 * BS), F32),
        pltpu.VMEM((PAIRS, rows, HQ, 2 * BS), BF16),
        pltpu.VMEM((rows, HQ, C), BF16),
        pltpu.VMEM((rows, HQ, C), BF16),
        pltpu.VMEM((rows, 2, 64, 256), BF16),
        pltpu.VMEM((rows, 2, 64, 256), BF16),
        pltpu.VMEM((rows, HQ, 128), F32),
        pltpu.VMEM((rows, HQ, 256), F32),
        pltpu.VMEM((rows, HQ, 128), F32),
        pltpu.VMEM((rows, HQ, C), F32),
        pltpu.VMEM((HQ * TAB, BS), F32),
    ]
    sum_type = BF16 if last else F32
    return pl.pallas_call(
        functools.partial(attention_kernel, rows, last),
        out_shape=(
            jax.ShapeDtypeStruct((BS, width), BF16),
            jax.ShapeDtypeStruct((BS, width), BF16),
            jax.ShapeDtypeStruct((PAIRS, HQ, 2 * BS), BF16),
            jax.ShapeDtypeStruct((blocks, width, BS), sum_type),
            jax.ShapeDtypeStruct((blocks, width, BS), sum_type),
        ),
        grid=(1,),
        in_specs=[smem] * 3 + [block] * 3 + [vmem] * 2 + [bias_block] + [vmem] * len(sums),
        out_specs=[vmem] * 5,
        scratch_shapes=scratch + ([acc, acc] if last else []),
        compiler_params=pltpu.CompilerParams(vmem_limit_bytes=56 * 1024 * 1024),
        cost_estimate=pl.CostEstimate(
            flops=6 * 2 * rows * HQ * TAB * BS * 256,
            bytes_accessed=12 * 1024 * 1024,
            transcendentals=rows * HQ * TAB * BS,
        ),
    )(tab_k, tab_v, count, q, g, c, k, v, b, *sums)


def exchange(x, bit, size):
    return lax.ppermute(x, "col", [(d, d ^ bit) for d in range(size)])


def gather(x, order, size):
    for bit in order:
        x = jnp.concatenate([x, exchange(x, bit, size)], 0)
    return x


def combine_kernel(n, order_k, order_v, share, local, *refs):
    x, refs = refs[:local], refs[local:]
    (dk, dv, bias_out, dk_out, dv_out), refs = refs[:5], refs[5:]
    (send, recv, total, send_sem, recv_sem, chain_send, chain_recv), refs = refs[:7], refs[7:]
    steps = len(order_k)
    got_k, refs = refs[:steps], refs[steps:]
    got_v, refs = refs[:steps], refs[steps:]
    sum_k, refs = refs[: steps - 1], refs[steps - 1 :]
    sum_v = refs
    sum_k, sum_v = list(sum_k) + [dk_out], list(sum_v) + [dv_out]
    me = lax.axis_index("row")
    col = lax.axis_index("col")

    def partner(bit):
        return col + bit - 2 * bit * ((col // bit) % 2)

    barrier = pltpu.get_barrier_semaphore()

    @pl.when(me > 0)
    def _():
        pl.semaphore_signal(barrier, inc=1, device_id={"row": me - 1}, device_id_type=MESH)

    @pl.when(me < n - 1)
    def _():
        pl.semaphore_signal(barrier, inc=1, device_id={"row": me + 1}, device_id_type=MESH)

    for bit in order_k:
        pl.semaphore_signal(barrier, inc=1, device_id={"col": partner(bit)}, device_id_type=MESH)

    edge = (me == 0) | (me == n - 1)

    @pl.when(edge)
    def _():
        pl.semaphore_wait(barrier, steps + 1)

    @pl.when(jnp.logical_not(edge))
    def _():
        pl.semaphore_wait(barrier, steps + 2)

    def bias_copy(j, d, s):
        return pltpu.make_async_remote_copy(
            src_ref=send.at[j, d, s],
            dst_ref=recv.at[j, d, s],
            send_sem=send_sem.at[j, d, s],
            recv_sem=recv_sem.at[j, d, s],
            device_id={"row": (me + (n - 1 if d == 0 else 1)) % n},
            device_id_type=MESH,
        )

    def chain_copy(kind, s):
        order, got, sums, own = ((order_k, got_k, sum_k, dk), (order_v, got_v, sum_v, dv))[kind]
        src = own if s == 0 else sums[s - 1]
        half = src.shape[0] // 2
        copy = pltpu.make_async_remote_copy(
            src_ref=src.at[pl.ds(half, half)],
            dst_ref=got[s],
            send_sem=chain_send.at[kind, s],
            recv_sem=chain_recv.at[kind, s],
            device_id={"col": partner(order[::-1][s])},
            device_id_type=MESH,
        )
        return copy, src, half, got[s], sums[s]

    def depth_of(d):
        return me if d == 0 else n - 1 - me

    def part(j, owner):
        return x[j][pl.ds(owner * share, share)]

    def bias_step(s):
        for j in range(local):
            for d in range(2):
                depth = depth_of(d)
                owner = me + s - (n - 1) if d == 0 else me + (n - 1) - s

                @pl.when(depth == n - 1)
                def _():
                    send[j, d, s] = part(j, owner)
                    bias_copy(j, d, s).start()

                if s > 0:

                    @pl.when((depth >= n - 1 - s) & (depth < n - 1))
                    def _():
                        bias_copy(j, d, s - 1).wait_recv()
                        mine = part(j, owner).astype(F32)
                        send[j, d, s] = (mine + recv[j, d, s - 1].astype(F32)).astype(BF16)
                        bias_copy(j, d, s).start()

    bias_step(0)
    for kind in range(2):
        chain_copy(kind, 0)[0].start()
    for s in range(steps):
        for kind in range(2):
            copy, src, half, got, dst = chain_copy(kind, s)
            copy.wait_recv()
            dst[...] = (src[:half].astype(F32) + got[...].astype(F32)).astype(BF16)
            if s + 1 < steps:
                chain_copy(kind, s + 1)[0].start()
    for s in range(1, n - 1):
        bias_step(s)
    for j in range(local):
        total[...] = part(j, me).astype(F32)
        for d in range(2):

            @pl.when(depth_of(d) < n - 1)
            def _():
                bias_copy(j, d, n - 2).wait_recv()
                total[...] += recv[j, d, n - 2].astype(F32)

        bias_out[j] = total[...].astype(BF16)
    for s in range(steps):
        for kind in range(2):
            chain_copy(kind, s)[0].wait_send()
    for s in range(n - 1):
        for j in range(local):
            for d in range(2):

                @pl.when(depth_of(d) >= n - 1 - s)
                def _():
                    bias_copy(j, d, s).wait_send()


def combine(terms, dk, dv, order_k, order_v):
    n = lax.axis_size("row")
    local = len(terms)
    share = terms[0].shape[0] // n
    steps = len(order_k)
    tail = terms[0].shape[1:]
    vmem = pl.BlockSpec(memory_space=pltpu.VMEM)
    halves = [pltpu.VMEM((dk.shape[0] >> (s + 1),) + dk.shape[1:], BF16) for s in range(steps)]
    small = jax.ShapeDtypeStruct((dk.shape[0] >> steps,) + dk.shape[1:], BF16)
    slots = pltpu.VMEM((local, 2, n - 1, share) + tail, BF16)
    sems = pltpu.SemaphoreType.DMA((local, 2, n - 1))
    chain_sems = pltpu.SemaphoreType.DMA((2, steps))
    return pl.pallas_call(
        functools.partial(combine_kernel, n, order_k, order_v, share, local),
        out_shape=(jax.ShapeDtypeStruct((local, share) + tail, BF16), small, small),
        in_specs=[vmem] * (local + 2),
        out_specs=[vmem] * 3,
        scratch_shapes=[
            slots, slots, pltpu.VMEM((share,) + tail, F32), sems, sems, chain_sems, chain_sems,
        ] + halves * 2 + halves[:-1] * 2,
        compiler_params=pltpu.CompilerParams(
            collective_id=0, has_side_effects=True, vmem_limit_bytes=48 * 1024 * 1024
        ),
    )(*terms, dk, dv)


def positions(blocks, order, me, per_device):
    apart = (blocks // per_device) ^ me
    place = jnp.zeros_like(apart)
    for rank, bit in enumerate(order):
        place = place + jnp.where((apart & bit) != 0, 1 << rank, 0)
    return place * per_device + blocks % per_device


def body(q, k, v, g, c, pair_bias, block_table, valid_counts):
    length, rows, channels = q.shape
    local = length // BS
    width = rows * channels
    size = lax.axis_size("col")
    me = lax.axis_index("col")
    bits = [1 << n for n in range(size.bit_length() - 1)]
    order_k = bits[1:] + bits[:1]
    order_v = bits[1:][::-1] + bits[:1]
    k_all = gather(k.reshape(local, BS, width), order_k, size)
    v_all = gather(v.reshape(local, BS, width), order_v, size)
    tab_k = positions(block_table, order_k, me, local)
    tab_v = positions(block_table, order_v, me, local)
    q, g, c = (x.reshape(local, BS, width) for x in (q, g, c))
    sums = ()
    dqs, ggs, terms = [], [], []
    for j in range(local):
        dq, gg, bg, *sums = attention(
            rows, j, j == local - 1, tab_k[j], tab_v[j], valid_counts[j : j + 1],
            q, g, c, k_all, v_all, pair_bias, sums,
        )
        dqs.append(dq)
        ggs.append(gg)
        terms.append(bg)
    biases, dk, dv = combine(terms, sums[0], sums[1], order_k, order_v)

    def leave(x):
        return x.transpose(0, 2, 1).reshape(length, rows, channels)

    own = biases.shape[1]
    bias_grad = biases.reshape(local, own, H, BS, 2, BS)
    bias_grad = bias_grad.transpose(0, 2, 3, 1, 4, 5).reshape(local, H, BS, own * 2, BS)
    return (
        jnp.concatenate(dqs, 0).reshape(length, rows, channels),
        leave(dk),
        leave(dv),
        jnp.concatenate(ggs, 0).reshape(length, rows, channels),
        bias_grad,
    )


def solution(mesh):
    split = P("col", "row", None)
    bias = P("col", None, None, None, None)
    return jax.shard_map(
        body,
        mesh=mesh,
        in_specs=(split,) * 5 + (bias, P("col", None), P("col")),
        out_specs=(split,) * 4 + (P("col", None, None, "row", None),),
        check_vma=False,
    )
```

```python
import functools

import jax
import jax.numpy as jnp
from jax import lax
from jax.experimental import pallas as pl
from jax.experimental.pallas import tpu as pltpu
from jax.sharding import PartitionSpec as P

H = 4
DH = 32
BS = 128
TAB = 16
PAIRS = TAB // 2
C = H * DH
HQ = H * BS
SCALE = DH ** (-0.5)
LOG2E = 1.4426950408889634
F32 = jnp.float32
BF16 = jnp.bfloat16
MESH = pl.DeviceIdType.MESH
NT = (((1,), (1,)), ((), ()))
NN = (((1,), (0,)), ((), ()))


def dot(a, b, dims=NN):
    return lax.dot_general(a, b, dims, preferred_element_type=F32)


def attention_kernel(rows, last, *refs):
    (tab_k, tab_v, count, q_ref, g_ref, c_ref, k_ref, v_ref, b_ref), refs = refs[:9], refs[9:]
    if last:
        (dk_in, dv_in), refs = refs[:2], refs[2:]
    (dq_ref, gg_ref, bg_ref, dk_out, dv_out), refs = refs[:5], refs[5:]
    s_ref, e_ref, qm, cm, qt, ct, mx, att, off, dqa, bias_ref = refs[:11]
    if last:
        dk_ref, dv_ref = refs[11:]
        dk_ref[...] = dk_in[...]
        dv_ref[...] = dv_in[...]
    else:
        dk_ref, dv_ref = dk_out, dv_out
        dk_ref[...] = jnp.zeros_like(dk_ref)
        dv_ref[...] = jnp.zeros_like(dv_ref)
    valid = count[0]
    pairs = (valid + 1) // 2
    lane_head = lax.broadcasted_iota(jnp.int32, (BS, C), 1) // DH

    def per_head(x):
        return jnp.concatenate([jnp.where(lane_head == h, x, 0.0) for h in range(H)], 0)

    def merge_heads(x):
        total = jnp.zeros((BS, C), F32)
        for h in range(H):
            total = jnp.where(lane_head == h, x[h * BS : (h + 1) * BS], total)
        return total

    def store_transposed(dst, i, x):
        for hp in range(2):
            turned = jnp.transpose(x[hp * 256 : (hp + 1) * 256])
            dst[i, hp] = turned[hp * 64 : (hp + 1) * 64].astype(BF16)

    def two(ref, tab, p, i):
        lanes = slice(i * C, (i + 1) * C)
        return jnp.concatenate([ref[tab[2 * p], :, lanes], ref[tab[2 * p + 1], :, lanes]], 0)

    def wide(x):
        return jnp.concatenate([x, x], 1)

    for h in range(H):
        span = slice(h * BS * TAB, (h + 1) * BS * TAB)
        bias_ref[span] = b_ref[h].reshape(BS * TAB, BS).astype(F32) * LOG2E

    for i in range(rows):
        q_heads = per_head(q_ref[:, i * C : (i + 1) * C].astype(F32))
        qm[i] = q_heads.astype(BF16)
        store_transposed(qt, i, q_heads)
        mx[i] = jnp.full((HQ, 128), -jnp.inf, F32)
        att[i] = jnp.zeros((HQ, 256), F32)
        dqa[i] = jnp.zeros((HQ, C), F32)

    @pl.loop(0, pairs)
    def _(p):
        lane_slot = lax.broadcasted_iota(jnp.int32, (1, 2 * BS), 1) // BS
        shut = jnp.where(2 * p + lane_slot < valid, 0.0, -jnp.inf)
        first = bias_ref[pl.ds(2 * p, HQ, stride=TAB), :]
        second = bias_ref[pl.ds(2 * p + 1, HQ, stride=TAB), :]
        bias = jnp.concatenate([first, second], 1) + shut
        for i in range(rows):
            raw = dot(qm[i], two(k_ref, tab_k, p, i), NT)
            s = raw * (SCALE * LOG2E) + bias
            s_ref[p, i] = s
            mx[i] = jnp.maximum(mx[i], jnp.maximum(s[:, :BS], s[:, BS:]))

    for i in range(rows):
        mx[i] = jnp.broadcast_to(jnp.max(mx[i], axis=1, keepdims=True), (HQ, 128))

    @pl.loop(0, pairs)
    def _(p):
        for i in range(rows):
            e = jnp.exp2(s_ref[p, i] - wide(mx[i])).astype(BF16)
            e_ref[p, i] = e
            values = jnp.concatenate([two(v_ref, tab_v, p, i), jnp.ones((2 * BS, C), BF16)], 1)
            att[i] += dot(e, values)

    for i in range(rows):
        lanes = slice(i * C, (i + 1) * C)
        inverse = 1.0 / att[i, :, C:]
        attended = att[i, :, :C] * inverse
        opened = jax.nn.sigmoid(g_ref[:, lanes].astype(F32))
        upstream = c_ref[:, lanes].astype(F32)
        gg_ref[:, lanes] = (upstream * merge_heads(attended) * opened * (1.0 - opened)).astype(BF16)
        core = (upstream * opened).astype(BF16).astype(F32)
        core_scaled = (per_head(core) * inverse).astype(BF16)
        cm[i] = core_scaled
        scaled = core_scaled.astype(F32)
        store_transposed(ct, i, scaled)
        off[i] = jnp.broadcast_to(jnp.sum(scaled * attended, axis=1, keepdims=True), (HQ, 128))

    @pl.loop(0, pairs)
    def _(p):
        total = None
        for i in range(rows):
            keys = two(k_ref, tab_k, p, i)
            dw = dot(cm[i], two(v_ref, tab_v, p, i), NT)
            e = e_ref[p, i]
            ds = e.astype(F32) * (dw - wide(off[i]))
            total = ds if total is None else total + ds
            half = ds.astype(BF16)
            dqa[i] += dot(half, keys)
            for hp in range(2):
                span = slice(hp * 256, (hp + 1) * 256)
                dst = slice(i * C + hp * 64, i * C + (hp + 1) * 64)
                key_term = dot(qt[i, hp], half[span])
                value_term = dot(ct[i, hp], e[span])
                for slot in range(2):
                    part = slice(slot * BS, (slot + 1) * BS)
                    dk_ref[tab_k[2 * p + slot], dst, :] += key_term[:, part]
                    dv_ref[tab_v[2 * p + slot], dst, :] += value_term[:, part]
        bg_ref[p] = total.astype(BF16)

    @pl.loop(pairs, PAIRS)
    def _(p):
        bg_ref[p] = jnp.zeros((HQ, 2 * BS), BF16)

    for i in range(rows):
        dq_ref[:, i * C : (i + 1) * C] = (merge_heads(dqa[i]) * SCALE).astype(BF16)
    if last:

        @pl.loop(0, dk_ref.shape[0])
        def _(b):
            dk_out[b] = (dk_ref[b] * SCALE).astype(BF16)
            dv_out[b] = dv_ref[b].astype(BF16)


def attention(rows, j, last, tab_k, tab_v, count, q, g, c, k, v, b, sums):
    blocks = k.shape[0]
    width = rows * C
    smem = pl.BlockSpec(memory_space=pltpu.SMEM)
    vmem = pl.BlockSpec(memory_space=pltpu.VMEM)
    block = pl.BlockSpec((None, BS, width), lambda n: (j, 0, 0))
    bias_block = pl.BlockSpec((None, H, BS, TAB, BS), lambda n: (j, 0, 0, 0, 0))
    acc = pltpu.VMEM((blocks, width, BS), F32)
    scratch = [
        pltpu.VMEM((PAIRS, rows, HQ, 2 * BS), F32),
        pltpu.VMEM((PAIRS, rows, HQ, 2 * BS), BF16),
        pltpu.VMEM((rows, HQ, C), BF16),
        pltpu.VMEM((rows, HQ, C), BF16),
        pltpu.VMEM((rows, 2, 64, 256), BF16),
        pltpu.VMEM((rows, 2, 64, 256), BF16),
        pltpu.VMEM((rows, HQ, 128), F32),
        pltpu.VMEM((rows, HQ, 256), F32),
        pltpu.VMEM((rows, HQ, 128), F32),
        pltpu.VMEM((rows, HQ, C), F32),
        pltpu.VMEM((HQ * TAB, BS), F32),
    ]
    sum_type = BF16 if last else F32
    return pl.pallas_call(
        functools.partial(attention_kernel, rows, last),
        out_shape=(
            jax.ShapeDtypeStruct((BS, width), BF16),
            jax.ShapeDtypeStruct((BS, width), BF16),
            jax.ShapeDtypeStruct((PAIRS, HQ, 2 * BS), BF16),
            jax.ShapeDtypeStruct((blocks, width, BS), sum_type),
            jax.ShapeDtypeStruct((blocks, width, BS), sum_type),
        ),
        grid=(1,),
        in_specs=[smem] * 3 + [block] * 3 + [vmem] * 2 + [bias_block] + [vmem] * len(sums),
        out_specs=[vmem] * 5,
        scratch_shapes=scratch + ([acc, acc] if last else []),
        compiler_params=pltpu.CompilerParams(vmem_limit_bytes=56 * 1024 * 1024),
        cost_estimate=pl.CostEstimate(
            flops=6 * 2 * rows * HQ * TAB * BS * 256,
            bytes_accessed=12 * 1024 * 1024,
            transcendentals=rows * HQ * TAB * BS,
        ),
    )(tab_k, tab_v, count, q, g, c, k, v, b, *sums)


def exchange(x, bit, size):
    return lax.ppermute(x, "col", [(d, d ^ bit) for d in range(size)])


def gather(x, order, size):
    for bit in order:
        x = jnp.concatenate([x, exchange(x, bit, size)], 0)
    return x


def combine_kernel(n, order_k, order_v, share, local, *refs):
    early, x, refs = refs[0], refs[1 : local + 1], refs[local + 1 :]
    (dk, dv, bias_out, dk_out, dv_out), refs = refs[:5], refs[5:]
    (send, recv, total, send_sem, recv_sem, chain_send, chain_recv), refs = refs[:7], refs[7:]
    steps = len(order_k)
    got_k, refs = refs[:steps], refs[steps:]
    got_v, refs = refs[:steps], refs[steps:]
    sum_k, refs = refs[: steps - 1], refs[steps - 1 :]
    sum_v = refs
    sum_k, sum_v = list(sum_k) + [dk_out], list(sum_v) + [dv_out]
    me = lax.axis_index("row")
    col = lax.axis_index("col")

    def partner(bit):
        return col + bit - 2 * bit * ((col // bit) % 2)

    barrier = pltpu.get_barrier_semaphore()

    @pl.when(me > 0)
    def _():
        pl.semaphore_signal(barrier, inc=1, device_id={"row": me - 1}, device_id_type=MESH)

    @pl.when(me < n - 1)
    def _():
        pl.semaphore_signal(barrier, inc=1, device_id={"row": me + 1}, device_id_type=MESH)

    for bit in order_k:
        pl.semaphore_signal(barrier, inc=1, device_id={"col": partner(bit)}, device_id_type=MESH)

    edge = (me == 0) | (me == n - 1)

    @pl.when(edge)
    def _():
        pl.semaphore_wait(barrier, steps + 1)

    @pl.when(jnp.logical_not(edge))
    def _():
        pl.semaphore_wait(barrier, steps + 2)

    def bias_copy(j, d, s):
        return pltpu.make_async_remote_copy(
            src_ref=send.at[j, d, s],
            dst_ref=recv.at[j, d, s],
            send_sem=send_sem.at[j, d, s],
            recv_sem=recv_sem.at[j, d, s],
            device_id={"row": (me + (n - 1 if d == 0 else 1)) % n},
            device_id_type=MESH,
        )

    def chain_copy(kind, s):
        order, got, sums, own = ((order_k, got_k, sum_k, dk), (order_v, got_v, sum_v, dv))[kind]
        src = own if s == 0 else sums[s - 1]
        half = src.shape[0] // 2
        copy = pltpu.make_async_remote_copy(
            src_ref=src.at[pl.ds(half, half)],
            dst_ref=got[s],
            send_sem=chain_send.at[kind, s],
            recv_sem=chain_recv.at[kind, s],
            device_id={"col": partner(order[::-1][s])},
            device_id_type=MESH,
        )
        return copy, src, half, got[s], sums[s]

    def depth_of(d):
        return me if d == 0 else n - 1 - me

    def receive(j, d, s):
        if (j, s) == (0, 0):
            return early[...].astype(F32)
        bias_copy(j, d, s).wait_recv()
        return recv[j, d, s].astype(F32)

    def part(j, owner):
        return x[j][pl.ds(owner * share, share)]

    def bias_step(s):
        for j in range(1 if s == 0 else 0, local):
            for d in range(2):
                depth = depth_of(d)
                owner = me + s - (n - 1) if d == 0 else me + (n - 1) - s

                @pl.when(depth == n - 1)
                def _():
                    send[j, d, s] = part(j, owner)
                    bias_copy(j, d, s).start()

                if s > 0:

                    @pl.when((depth >= n - 1 - s) & (depth < n - 1))
                    def _():
                        mine = part(j, owner).astype(F32)
                        send[j, d, s] = (mine + receive(j, d, s - 1)).astype(BF16)
                        bias_copy(j, d, s).start()

    bias_step(0)
    for kind in range(2):
        chain_copy(kind, 0)[0].start()
    for s in range(steps):
        for kind in range(2):
            copy, src, half, got, dst = chain_copy(kind, s)
            copy.wait_recv()
            dst[...] = (src[:half].astype(F32) + got[...].astype(F32)).astype(BF16)
            if s + 1 < steps:
                chain_copy(kind, s + 1)[0].start()
    for s in range(1, n - 1):
        bias_step(s)
    for j in range(local):
        total[...] = part(j, me).astype(F32)
        for d in range(2):

            @pl.when(depth_of(d) < n - 1)
            def _():
                total[...] += receive(j, d, n - 2)

        bias_out[j] = total[...].astype(BF16)
    for s in range(steps):
        for kind in range(2):
            chain_copy(kind, s)[0].wait_send()
    for s in range(n - 1):
        for j in range(1 if s == 0 else 0, local):
            for d in range(2):

                @pl.when(depth_of(d) >= n - 1 - s)
                def _():
                    bias_copy(j, d, s).wait_send()


def ends_first(x):
    n = lax.axis_size("row")
    share = x.shape[0] // n
    start = jnp.where(lax.axis_index("row") == 0, (n - 1) * share, 0)
    chunk = lax.dynamic_slice_in_dim(x, start, share, 0)
    return lax.ppermute(chunk, "row", [(n - 1, n - 2), (0, 1)])


def combine(early, terms, dk, dv, order_k, order_v):
    n = lax.axis_size("row")
    local = len(terms)
    share = terms[0].shape[0] // n
    steps = len(order_k)
    tail = terms[0].shape[1:]
    vmem = pl.BlockSpec(memory_space=pltpu.VMEM)
    halves = [pltpu.VMEM((dk.shape[0] >> (s + 1),) + dk.shape[1:], BF16) for s in range(steps)]
    small = jax.ShapeDtypeStruct((dk.shape[0] >> steps,) + dk.shape[1:], BF16)
    slots = pltpu.VMEM((local, 2, n - 1, share) + tail, BF16)
    sems = pltpu.SemaphoreType.DMA((local, 2, n - 1))
    chain_sems = pltpu.SemaphoreType.DMA((2, steps))
    return pl.pallas_call(
        functools.partial(combine_kernel, n, order_k, order_v, share, local),
        out_shape=(jax.ShapeDtypeStruct((local, share) + tail, BF16), small, small),
        in_specs=[vmem] * (local + 3),
        out_specs=[vmem] * 3,
        scratch_shapes=[
            slots, slots, pltpu.VMEM((share,) + tail, F32), sems, sems, chain_sems, chain_sems,
        ] + halves * 2 + halves[:-1] * 2,
        compiler_params=pltpu.CompilerParams(
            collective_id=0, has_side_effects=True, vmem_limit_bytes=48 * 1024 * 1024
        ),
    )(early, *terms, dk, dv)


def positions(blocks, order, me, per_device):
    apart = (blocks // per_device) ^ me
    place = jnp.zeros_like(apart)
    for rank, bit in enumerate(order):
        place = place + jnp.where((apart & bit) != 0, 1 << rank, 0)
    return place * per_device + blocks % per_device


def body(q, k, v, g, c, pair_bias, block_table, valid_counts):
    length, rows, channels = q.shape
    local = length // BS
    width = rows * channels
    size = lax.axis_size("col")
    me = lax.axis_index("col")
    bits = [1 << n for n in range(size.bit_length() - 1)]
    order_k = bits[1:] + bits[:1]
    order_v = bits[1:][::-1] + bits[:1]
    k_all = gather(k.reshape(local, BS, width), order_k, size)
    v_all = gather(v.reshape(local, BS, width), order_v, size)
    tab_k = positions(block_table, order_k, me, local)
    tab_v = positions(block_table, order_v, me, local)
    q, g, c = (x.reshape(local, BS, width) for x in (q, g, c))
    sums = ()
    dqs, ggs, terms = [], [], []
    for j in range(local):
        dq, gg, bg, *sums = attention(
            rows, j, j == local - 1, tab_k[j], tab_v[j], valid_counts[j : j + 1],
            q, g, c, k_all, v_all, pair_bias, sums,
        )
        dqs.append(dq)
        ggs.append(gg)
        terms.append(bg)
        if j == 0:
            early = ends_first(bg)
    biases, dk, dv = combine(early, terms, sums[0], sums[1], order_k, order_v)

    def leave(x):
        return x.transpose(0, 2, 1).reshape(length, rows, channels)

    own = biases.shape[1]
    bias_grad = biases.reshape(local, own, H, BS, 2, BS)
    bias_grad = bias_grad.transpose(0, 2, 3, 1, 4, 5).reshape(local, H, BS, own * 2, BS)
    return (
        jnp.concatenate(dqs, 0).reshape(length, rows, channels),
        leave(dk),
        leave(dv),
        jnp.concatenate(ggs, 0).reshape(length, rows, channels),
        bias_grad,
    )


def solution(mesh):
    split = P("col", "row", None)
    bias = P("col", None, None, None, None)
    return jax.shard_map(
        body,
        mesh=mesh,
        in_specs=(split,) * 5 + (bias, P("col", None), P("col")),
        out_specs=(split,) * 4 + (P("col", None, None, "row", None),),
        check_vma=False,
    )
```
